256 devices in a mesh: row: 8 (over z), col: 32 (over y, x, core).
Axes of the slice: x: 4, y: 4, z: 8, core: 2. Of those that a mesh axis runs over, the one named last changes fastest.
Arguments:
- tokens: bfloat16 [1024, 8192], P('col', 'row'), may hold values from -6 to 6
- modality: int32 [1024], P('row'), may hold values 0 or 1
- in_weight: bfloat16 [8192, 2, 28672], P('row', None, 'col'), may hold values from -0.0625 to 0.0625
- down_weight: bfloat16 [28672, 8192], P('col', 'row'), may hold values from -0.03125 to 0.03125
- d_mixed: bfloat16 [1024, 8192], P('col', 'row'), may hold values from -6 to 6
Outputs:
- mixed: bfloat16 [1024, 8192], P('col', 'row')
- d_down: bfloat16 [28672, 8192], P('col', 'row')
- d_in: bfloat16 [8192, 2, 28672], P('row', None, 'col')
- d_tokens: bfloat16 [1024, 8192], P('col', 'row')
The draws below stay inside these ranges and needn't reach their ends.
All inputs are finite; a program needn't handle non-finite values. No bound on the sum of `modality` on one device may be relied on, other than what follows from the above.
Results may differ from the reference program's by a relative error of at most 0.0049.
Values may be sent and summed in bfloat16 or wider, within the bound.
No kernel may reach another device: no remote copies, remote signals or barrier semaphores. Data moves between devices by JAX's collectives and lax.ppermute only.
A program may use at most 128 MiB of HBM per device.

```python
import jax
import jax.numpy as jnp

D = 8192
FF = 28672
TOKENS = 1024


def touch_ends(result, rng, least, top_value):
    index_at = [jax.random.randint(jax.random.fold_in(rng, axis), (), 0, length) for axis, length in enumerate(result.shape)]
    longest = result.shape.index(max(result.shape))
    next_to = index_at[:longest] + [(index_at[longest] + 1) % result.shape[longest]] + index_at[longest + 1:]
    return result.at[tuple(index_at)].set(least).at[tuple(next_to)].set(top_value)


def block_levels(key, shape, cuts, low, high):
    factor_of, own = 1.0, jax.random.fold_in(key, 6)
    for position, shards_of in cuts:
        steps = jnp.exp(jax.random.uniform(jax.random.fold_in(own, position), (shards_of,), jnp.float32, low / len(cuts), high / len(cuts)))
        factor_of = factor_of * jnp.repeat(steps, shape[position] // shards_of).reshape([-1 if axis == position else 1 for axis in range(len(shape))])
    return factor_of


def noise(key, shape, scale, bound, split=(), held_as=jnp.bfloat16):
    drawn = scale * jax.random.normal(key, shape, jnp.float32)
    if split:
        drawn = drawn * block_levels(key, shape, split, -0.22, 0.18)
    return jnp.clip(drawn, -bound, bound).astype(held_as)


def setup_inputs(seed: int = 0) -> dict:
    key_of = jax.random.split(jax.random.key(seed), 6)
    tokens = noise(key_of[0], (TOKENS, D), 1.0, 6.0, ((0, 32), (1, 8)))
    modality = touch_ends((jax.random.randint(key_of[1], (TOKENS,), 0, 2) < 1).astype(jnp.int32), jax.random.fold_in(key_of[1], 1), 0, 1)
    in_weight = noise(key_of[2], (D, 2, FF), D ** -0.5, 0.0625, ((0, 8), (2, 32)))
    down_weight = noise(key_of[3], (FF, D), FF ** -0.5, 0.03125, ((0, 32), (1, 8)))
    d_mixed = noise(key_of[4], (TOKENS, D), 1.0, 6.0, ((0, 32), (1, 8)))
    return {"tokens": tokens, "modality": modality, "in_weight": in_weight, "down_weight": down_weight, "d_mixed": d_mixed}


def reference(tokens, modality, in_weight, down_weight, d_mixed):
    selected = (modality == 1).astype(jnp.float32)[:, None]
    flat_in = in_weight.reshape(D, 2 * FF)
    projected = jnp.dot(tokens, flat_in, preferred_element_type=jnp.float32)
    gate_part = projected[:, :FF]
    up_part = projected[:, FF:]
    sigmoid_gate = jax.nn.sigmoid(gate_part)
    activated = gate_part * sigmoid_gate
    hidden = (selected * activated * up_part).astype(jnp.bfloat16)
    mixed = jnp.dot(hidden, down_weight, preferred_element_type=jnp.float32).astype(jnp.bfloat16)
    d_down = jnp.dot(hidden.T, d_mixed, preferred_element_type=jnp.float32).astype(jnp.bfloat16)
    d_hidden = jnp.dot(d_mixed, down_weight.T, preferred_element_type=jnp.float32)
    d_scaled = selected * d_hidden
    d_gate = d_scaled * up_part * (sigmoid_gate + gate_part * sigmoid_gate * (1.0 - sigmoid_gate))
    d_up = d_scaled * activated
    d_projected = jnp.concatenate([d_gate, d_up], 1).astype(jnp.bfloat16)
    d_in = jnp.dot(tokens.T, d_projected, preferred_element_type=jnp.float32).reshape(D, 2, FF).astype(jnp.bfloat16)
    d_tokens = jnp.dot(d_projected, flat_in.T, preferred_element_type=jnp.float32).astype(jnp.bfloat16)
    return mixed, d_down, d_in, d_tokens
```

```python
import jax
import jax.numpy as jnp
from jax import lax
from jax.sharding import PartitionSpec as P

BF16 = jnp.bfloat16
F32 = jnp.float32


def positions(modality):
    flags = lax.all_gather((modality == 1).astype(BF16), "row", axis=0)
    rows, width = flags.shape
    upto = lax.broadcasted_iota(jnp.int32, (width, width), 0) <= lax.broadcasted_iota(
        jnp.int32, (width, width), 1
    )
    within = jnp.dot(flags, upto.astype(BF16), preferred_element_type=F32)
    totals = jnp.sum(flags.astype(F32), axis=1)
    before = jnp.cumsum(totals) - totals
    place = jnp.where(flags > 0, within + before[:, None] - 1.0, -1.0)
    return place.astype(jnp.int32).reshape(1, rows * width), jnp.sum(totals)


def col_sum_scatter(part):
    cols = lax.psum(1, "col")
    got = lax.all_to_all(part, "col", 0, 0, tiled=True)
    got = got.reshape(cols, part.shape[0] // cols, part.shape[1])
    return jnp.sum(got.astype(F32), axis=0).astype(BF16)


def block(capacity, place, rows_all, cotangent_all, in_weight, down_weight):
    width = in_weight.shape[2]
    flat_in = in_weight.reshape(in_weight.shape[0], 2 * width)
    pick = (
        lax.broadcasted_iota(jnp.int32, (capacity, place.shape[1]), 0) == place
    ).astype(BF16)
    rows = jnp.dot(pick, rows_all)
    cotangent = jnp.dot(pick, cotangent_all)
    projected = lax.psum_scatter(
        jnp.dot(rows, flat_in, preferred_element_type=F32), "row", scatter_dimension=0, tiled=True
    )
    d_hidden = lax.psum_scatter(
        jnp.einsum("td,fd->tf", cotangent, down_weight, preferred_element_type=F32),
        "row",
        scatter_dimension=0,
        tiled=True,
    )
    gate, up = projected[:, :width], projected[:, width:]
    sig = jax.nn.sigmoid(gate)
    activated = gate * sig
    hidden = (activated * up).astype(BF16)
    d_gate = (d_hidden * up * (sig + gate * sig * (1.0 - sig))).astype(BF16)
    d_up = (d_hidden * activated).astype(BF16)
    hidden_all = lax.all_gather(hidden, "row", axis=0, tiled=True)
    d_projected = lax.all_gather(
        jnp.concatenate([d_gate, d_up], 1), "row", axis=0, tiled=True
    )
    mixed = jnp.dot(hidden_all, down_weight, preferred_element_type=F32).astype(BF16)
    mixed = col_sum_scatter(jnp.einsum("kt,kd->td", pick, mixed))
    d_tokens = jnp.einsum("tk,dk->td", d_projected, flat_in, preferred_element_type=F32).astype(BF16)
    d_tokens = col_sum_scatter(jnp.einsum("kt,kd->td", pick, d_tokens))
    d_down = jnp.einsum("tf,td->fd", hidden_all, cotangent, preferred_element_type=F32).astype(BF16)
    d_in = jnp.einsum("td,tk->dk", rows, d_projected, preferred_element_type=F32).astype(BF16)
    return mixed, d_down, d_in.reshape(in_weight.shape), d_tokens


def per_device(tokens, modality, in_weight, down_weight, d_mixed):
    place, count = positions(modality)
    features = tokens.shape[1]
    both = lax.all_gather(jnp.concatenate([tokens, d_mixed], 1), "col", axis=0, tiled=True)
    rows_all, cotangent_all = both[:, :features], both[:, features:]
    total = rows_all.shape[0]
    some = total // 16 * 9
    operands = (place, rows_all, cotangent_all, in_weight, down_weight)
    return lax.cond(
        count <= some,
        lambda args: block(some, *args),
        lambda args: block(total, *args),
        operands,
    )


def solution(mesh):
    return jax.shard_map(
        per_device,
        mesh=mesh,
        in_specs=(
            P("col", "row"),
            P("row"),
            P("row", None, "col"),
            P("col", "row"),
            P("col", "row"),
        ),
        out_specs=(P("col", "row"), P("col", "row"), P("row", None, "col"), P("col", "row")),
        check_vma=False,
    )
```

```python
import jax
import jax.numpy as jnp
from jax import lax
from jax.sharding import PartitionSpec as P

BF16 = jnp.bfloat16
F32 = jnp.float32
SIDES = (4, 4, 2)


def after(array, *others):
    return lax.optimization_barrier((array,) + others)[0]


def col_shift(array, axis, step):
    moves = []
    for source in range(32):
        at = [source // 8, source // 2 % 4, source % 2]
        at[axis] = (at[axis] + step) % SIDES[axis]
        moves.append((source, at[0] * 8 + at[1] * 2 + at[2]))
    return lax.ppermute(array, "col", moves)


def row_shift(array, step):
    rows = lax.psum(1, "row")
    return lax.ppermute(array, "row", [(i, (i + step) % rows) for i in range(rows)])


def spread(array, axis):
    return jnp.stack([array] + [col_shift(array, axis, step) for step in (-1, 2, 1)])


def col_gather(array, beside):
    array = spread(spread(array, 0), 1)
    return jnp.stack([array, col_shift(after(array, beside), 2, 1)])


def row_gather(own):
    half = own.shape[1] // 256 * 128
    up, down = [own], [own]
    for _ in range(3):
        up.append(row_shift(up[-1], 1))
        down.append(row_shift(down[-1], -1))
    middle = jnp.concatenate(
        [row_shift(up[3][:, :half], 1), row_shift(down[3][:, half:], -1)], axis=1
    )
    return jnp.concatenate(down + [middle] + up[:0:-1], axis=0), up[1], down[1]


def row_sum_scatter(terms, long_up):
    size = terms.shape[0] // 8
    block = lambda b: terms[b * size : (b + 1) * size]

    def run(order, step):
        total, passed = block(order[0]), []
        for b in order[1:]:
            passed.append(row_shift(total.astype(BF16), step))
            total = passed[-1].astype(F32) + block(b)
        return row_shift(total, step), passed[0]

    up, early = run([4, 3, 2, 1] if long_up else [3, 2, 1], 1)
    down, _ = run([5, 6, 7] if long_up else [4, 5, 6, 7], -1)
    return block(0) + up + down, early


def positions(flags):
    rows, width = flags.shape
    upto = lax.broadcasted_iota(jnp.int32, (width, width), 0) <= lax.broadcasted_iota(
        jnp.int32, (width, width), 1
    )
    within = jnp.dot(flags, upto.astype(BF16), preferred_element_type=F32)
    totals = jnp.sum(flags.astype(F32), axis=1)
    before = jnp.cumsum(totals) - totals
    place = jnp.where(flags > 0, within + before[:, None] - 1.0, -1.0)
    return place.astype(jnp.int32).reshape(rows * width), jnp.sum(totals).astype(jnp.int32)


def col_order(place):
    grid = place.reshape(SIDES + (-1,))
    for axis in range(3):
        grid = jnp.concatenate([grid, grid], axis)
    me = lax.axis_index("col")
    grid = lax.dynamic_slice(grid, (me // 8, me // 2 % 4, me % 2, 0), SIDES + (grid.shape[3],))
    return grid.transpose(2, 1, 0, 3).reshape(-1)


def pick(wanted, place):
    return (wanted[:, None] == place[None, :]).astype(BF16)


def chip_sum(part, chosen):
    core = lax.axis_index("col") % 2
    half = part.shape[1] // 2
    other = lax.dynamic_slice(part, (0, (1 - core) * half), (part.shape[0], half))
    own = lax.dynamic_slice(part, (0, core * half), (part.shape[0], half))
    own = (own + col_shift(other, 2, 1)).astype(BF16)
    return jnp.einsum("kt,kd->td", chosen, own)


def owner_sum(spots, *beside):
    core = lax.axis_index("col") % 2
    chips = SIDES[0] * SIDES[1]
    groups = [[2 * chip + c for chip in range(chips)] for c in range(2)]
    got = lax.all_to_all(spots, "col", 0, 0, tiled=True, axis_index_groups=groups)
    got = got.reshape(chips, 2, spots.shape[0] // chips // 2, spots.shape[1])
    got = jnp.sum(got.astype(F32), axis=0).astype(BF16)
    if beside:
        got = after(got, *beside)
    away = col_shift(lax.dynamic_index_in_dim(got, 1 - core, 0, False), 2, 1)
    own = lax.dynamic_index_in_dim(got, core, 0, False)
    return jnp.where(
        core == 0, jnp.concatenate([own, away], 1), jnp.concatenate([away, own], 1)
    )


def activations(gate, up):
    sig = jax.nn.sigmoid(gate)
    activated = gate * sig
    return sig, activated, (activated * up).astype(BF16)


def cotangents(gate, up, sig, activated, d_hidden):
    d_gate = (d_hidden * up * (sig + gate * sig * (1.0 - sig))).astype(BF16)
    return d_gate, (d_hidden * activated).astype(BF16)


def sum_scatter(terms):
    return lax.psum_scatter(terms, "row", scatter_dimension=0, tiled=True)


def gather(own):
    return lax.all_gather(own, "row", axis=0, tiled=True)


def per_device(tokens, modality, in_weight, down_weight, d_mixed):
    width = in_weight.shape[2]
    flat_in = in_weight.reshape(in_weight.shape[0], 2 * width)
    features = tokens.shape[1]
    flags = lax.all_gather((modality == 1).astype(BF16), "row", axis=0)
    place, count = positions(flags)
    token_place = col_order(place)
    rows_all = col_gather(tokens, flags).reshape(-1, features)
    cotangent_all = lax.all_gather(d_mixed, "col", axis=0, tiled=True)
    total = rows_all.shape[0]
    some = total // 16 * 9

    wanted = lax.axis_index("row") * (some // 8) + lax.iota(jnp.int32, some)
    wanted = jnp.where(wanted >= some, wanted - some, wanted)
    rows = jnp.dot(pick(wanted, token_place), rows_all)
    gate, early_gate = row_sum_scatter(jnp.dot(rows, flat_in[:, :width], preferred_element_type=F32), True)
    up, early_up = row_sum_scatter(jnp.dot(rows, flat_in[:, width:], preferred_element_type=F32), False)
    cotangent_all = after(cotangent_all, early_gate, early_up)
    chosen = pick(wanted, place)
    canon = pick(lax.iota(jnp.int32, some), place)
    cotangent_canon = jnp.dot(canon, cotangent_all)
    d_hidden = sum_scatter(
        jnp.einsum("td,fd->tf", cotangent_canon, down_weight, preferred_element_type=F32)
    )
    sig, activated, hidden = activations(gate, up)
    hidden_all, *early_hidden = row_gather(hidden)
    d_hidden = after(d_hidden, *early_hidden)
    mixed_spots = chip_sum(jnp.dot(hidden_all, down_weight, preferred_element_type=F32), chosen)
    mixed = owner_sum(mixed_spots)
    cotangent = jnp.dot(chosen, cotangent_all)
    d_down = jnp.einsum("tf,td->fd", hidden_all, cotangent, preferred_element_type=F32).astype(BF16)
    d_gate, d_up = cotangents(gate, up, sig, activated, d_hidden)
    d_projected = gather(jnp.concatenate([d_gate, d_up], 1))
    d_projected = after(d_projected, mixed_spots, d_down)
    d_spots = chip_sum(
        jnp.einsum("tk,dk->td", d_projected, flat_in, preferred_element_type=F32), canon
    )
    canon_rows = jnp.dot(pick(lax.iota(jnp.int32, some), token_place), rows_all)
    d_in = jnp.einsum("td,tk->dk", canon_rows, d_projected, preferred_element_type=F32)
    d_in = d_in.reshape(in_weight.shape).astype(BF16)
    d_tokens = owner_sum(d_spots, d_in)

    rest = total - some

    def more(carry):
        return carry[0] < count

    def step(carry):
        start, mixed, d_down, d_in, d_tokens = carry
        wanted = start + lax.iota(jnp.int32, rest)
        chosen = pick(wanted, place)
        rows = jnp.dot(pick(wanted, token_place), rows_all)
        cotangent = jnp.dot(chosen, cotangent_all)
        projected = sum_scatter(jnp.dot(rows, flat_in, preferred_element_type=F32))
        d_hidden = sum_scatter(
            jnp.einsum("td,fd->tf", cotangent, down_weight, preferred_element_type=F32)
        )
        gate, up = projected[:, :width], projected[:, width:]
        sig, activated, hidden = activations(gate, up)
        d_projected = jnp.concatenate(cotangents(gate, up, sig, activated, d_hidden), 1)
        hidden, d_projected = gather(hidden), gather(d_projected)
        mixed += owner_sum(
            chip_sum(jnp.dot(hidden, down_weight, preferred_element_type=F32), chosen)
        )
        d_tokens += owner_sum(
            chip_sum(
                jnp.einsum("tk,dk->td", d_projected, flat_in, preferred_element_type=F32), chosen
            )
        )
        add = jnp.einsum("tf,td->fd", hidden, cotangent, preferred_element_type=F32)
        d_down = (d_down.astype(F32) + add).astype(BF16)
        add = jnp.einsum("td,tk->dk", rows, d_projected, preferred_element_type=F32)
        d_in = (d_in.astype(F32) + add.reshape(d_in.shape)).astype(BF16)
        return start + rest, mixed, d_down, d_in, d_tokens

    carry = (jnp.int32(some), mixed, d_down, d_in, d_tokens)
    return lax.while_loop(more, step, carry)[1:]


def solution(mesh):
    return jax.shard_map(
        per_device,
        mesh=mesh,
        in_specs=(
            P("col", "row"),
            P("row"),
            P("row", None, "col"),
            P("col", "row"),
            P("col", "row"),
        ),
        out_specs=(P("col", "row"), P("col", "row"), P("row", None, "col"), P("col", "row")),
        check_vma=False,
    )
```

```python
import jax
import jax.numpy as jnp
from jax import lax
from jax.sharding import PartitionSpec as P

BF16 = jnp.bfloat16
F32 = jnp.float32
SIDES = (4, 4, 2)


def after(array, *others):
    return lax.optimization_barrier((array,) + others)[0]


def col_shift(array, axis, step):
    moves = []
    for source in range(32):
        at = [source // 8, source // 2 % 4, source % 2]
        at[axis] = (at[axis] + step) % SIDES[axis]
        moves.append((source, at[0] * 8 + at[1] * 2 + at[2]))
    return lax.ppermute(array, "col", moves)


def row_shift(array, step):
    rows = lax.psum(1, "row")
    return lax.ppermute(array, "row", [(i, (i + step) % rows) for i in range(rows)])


def spread(array, axis):
    return jnp.stack([array] + [col_shift(array, axis, step) for step in (-1, 2, 1)])


def col_gather(array, beside):
    array = spread(spread(array, 0), 1)
    return jnp.stack([array, col_shift(after(array, beside), 2, 1)])


def row_gather(own):
    half = own.shape[1] // 256 * 128
    up, down = [own], [own]
    for _ in range(3):
        up.append(row_shift(up[-1], 1))
        down.append(row_shift(down[-1], -1))
    middle = jnp.concatenate(
        [row_shift(up[3][:, :half], 1), row_shift(down[3][:, half:], -1)], axis=1
    )
    return jnp.concatenate(down + [middle] + up[:0:-1], axis=0), up[1], down[1]


def row_sum_scatter(terms, long_up):
    size = terms.shape[0] // 8
    block = lambda b: terms[b * size : (b + 1) * size]

    def run(order, step):
        total, passed = block(order[0]), []
        for b in order[1:]:
            passed.append(row_shift(total.astype(BF16), step))
            total = passed[-1].astype(F32) + block(b)
        return row_shift(total, step), passed[0]

    up, early = run([4, 3, 2, 1] if long_up else [3, 2, 1], 1)
    down, _ = run([5, 6, 7] if long_up else [4, 5, 6, 7], -1)
    return block(0) + up + down, early


def positions(flags):
    rows, width = flags.shape
    upto = lax.broadcasted_iota(jnp.int32, (width, width), 0) <= lax.broadcasted_iota(
        jnp.int32, (width, width), 1
    )
    within = jnp.dot(flags, upto.astype(BF16), preferred_element_type=F32)
    totals = jnp.sum(flags.astype(F32), axis=1)
    before = jnp.cumsum(totals) - totals
    place = jnp.where(flags > 0, within + before[:, None] - 1.0, -1.0)
    return place.astype(jnp.int32).reshape(rows * width), jnp.sum(totals).astype(jnp.int32)


def col_order(place):
    grid = place.reshape(SIDES + (-1,))
    for axis in range(3):
        grid = jnp.concatenate([grid, grid], axis)
    me = lax.axis_index("col")
    grid = lax.dynamic_slice(grid, (me // 8, me // 2 % 4, me % 2, 0), SIDES + (grid.shape[3],))
    return grid.transpose(2, 1, 0, 3).reshape(-1)


def pick(wanted, place):
    return (wanted[:, None] == place[None, :]).astype(BF16)


def chip_sum(part, chosen):
    core = lax.axis_index("col") % 2
    half = part.shape[1] // 2
    other = lax.dynamic_slice(part, (0, (1 - core) * half), (part.shape[0], half))
    own = lax.dynamic_slice(part, (0, core * half), (part.shape[0], half))
    own = (own + col_shift(other, 2, 1)).astype(BF16)
    return jnp.einsum("kt,kd->td", chosen, own)


def owner_sum(spots, *beside):
    core = lax.axis_index("col") % 2
    chips = SIDES[0] * SIDES[1]
    groups = [[2 * chip + c for chip in range(chips)] for c in range(2)]
    got = lax.all_to_all(spots, "col", 0, 0, tiled=True, axis_index_groups=groups)
    got = got.reshape(chips, 2, spots.shape[0] // chips // 2, spots.shape[1])
    got = jnp.sum(got.astype(F32), axis=0).astype(BF16)
    if beside:
        got = after(got, *beside)
    away = col_shift(lax.dynamic_index_in_dim(got, 1 - core, 0, False), 2, 1)
    own = lax.dynamic_index_in_dim(got, core, 0, False)
    both = jnp.where(
        core == 0, jnp.concatenate([own, away], 1), jnp.concatenate([away, own], 1)
    )
    return both, got


def activations(gate, up):
    sig = jax.nn.sigmoid(gate)
    activated = gate * sig
    return sig, activated, (activated * up).astype(BF16)


def cotangents(gate, up, sig, activated, d_hidden):
    d_gate = (d_hidden * up * (sig + gate * sig * (1.0 - sig))).astype(BF16)
    return d_gate, (d_hidden * activated).astype(BF16)


def sum_scatter(terms):
    return lax.psum_scatter(terms, "row", scatter_dimension=0, tiled=True)


def gather(own):
    return lax.all_gather(own, "row", axis=0, tiled=True)


def per_device(tokens, modality, in_weight, down_weight, d_mixed):
    width = in_weight.shape[2]
    flat_in = in_weight.reshape(in_weight.shape[0], 2 * width)
    features = tokens.shape[1]
    flags = lax.all_gather((modality == 1).astype(BF16), "row", axis=0)
    place, count = positions(flags)
    token_place = col_order(place)
    rows_all = col_gather(tokens, flags).reshape(-1, features)
    cotangent_all = lax.all_gather(d_mixed, "col", axis=0, tiled=True)
    total = rows_all.shape[0]
    some = total // 16 * 9

    wanted = lax.axis_index("row") * (some // 8) + lax.iota(jnp.int32, some)
    wanted = jnp.where(wanted >= some, wanted - some, wanted)
    rows = jnp.dot(pick(wanted, token_place), rows_all)
    projected, early = row_sum_scatter(jnp.dot(rows, flat_in, preferred_element_type=F32), True)
    gate, up = projected[:, :width], projected[:, width:]
    cotangent_all = after(cotangent_all, early)
    chosen = pick(wanted, place)
    canon = pick(lax.iota(jnp.int32, some), place)
    d_hidden = sum_scatter(
        jnp.einsum(
            "td,fd->tf", jnp.dot(canon, cotangent_all), down_weight, preferred_element_type=F32
        )
    )
    sig, activated, hidden = activations(gate, up)
    hidden_all, *early_hidden = row_gather(hidden)
    d_hidden = after(d_hidden, *early_hidden)
    mixed_spots = chip_sum(jnp.dot(hidden_all, down_weight, preferred_element_type=F32), chosen)
    mixed, mixed_sum = owner_sum(mixed_spots)
    cotangent = jnp.dot(chosen, cotangent_all)
    d_down = jnp.einsum("tf,td->fd", hidden_all, cotangent, preferred_element_type=F32).astype(BF16)
    d_gate, d_up = cotangents(gate, up, sig, activated, d_hidden)
    d_projected = gather(jnp.concatenate([d_gate, d_up], 1))
    d_projected = after(d_projected, mixed_sum, d_down)
    d_spots = chip_sum(
        jnp.einsum("tk,dk->td", d_projected, flat_in, preferred_element_type=F32), canon
    )
    canon_rows = jnp.dot(pick(lax.iota(jnp.int32, some), token_place), rows_all)
    d_in = jnp.einsum("td,tk->dk", canon_rows, d_projected, preferred_element_type=F32)
    d_in = d_in.reshape(in_weight.shape).astype(BF16)
    d_tokens, _ = owner_sum(d_spots, d_in)

    rest = total - some

    def more(carry):
        return carry[0] < count

    def step(carry):
        start, mixed, d_down, d_in, d_tokens = carry
        wanted = start + lax.iota(jnp.int32, rest)
        chosen = pick(wanted, place)
        rows = jnp.dot(pick(wanted, token_place), rows_all)
        cotangent = jnp.dot(chosen, cotangent_all)
        projected = sum_scatter(jnp.dot(rows, flat_in, preferred_element_type=F32))
        d_hidden = sum_scatter(
            jnp.einsum("td,fd->tf", cotangent, down_weight, preferred_element_type=F32)
        )
        gate, up = projected[:, :width], projected[:, width:]
        sig, activated, hidden = activations(gate, up)
        d_projected = jnp.concatenate(cotangents(gate, up, sig, activated, d_hidden), 1)
        hidden, d_projected = gather(hidden), gather(d_projected)
        mixed += owner_sum(
            chip_sum(jnp.dot(hidden, down_weight, preferred_element_type=F32), chosen)
        )[0]
        d_tokens += owner_sum(
            chip_sum(
                jnp.einsum("tk,dk->td", d_projected, flat_in, preferred_element_type=F32), chosen
            )
        )[0]
        add = jnp.einsum("tf,td->fd", hidden, cotangent, preferred_element_type=F32)
        d_down = (d_down.astype(F32) + add).astype(BF16)
        add = jnp.einsum("td,tk->dk", rows, d_projected, preferred_element_type=F32)
        d_in = (d_in.astype(F32) + add.reshape(d_in.shape)).astype(BF16)
        return start + rest, mixed, d_down, d_in, d_tokens

    carry = (jnp.int32(some), mixed, d_down, d_in, d_tokens)
    return lax.while_loop(more, step, carry)[1:]


def solution(mesh):
    return jax.shard_map(
        per_device,
        mesh=mesh,
        in_specs=(
            P("col", "row"),
            P("row"),
            P("row", None, "col"),
            P("col", "row"),
            P("col", "row"),
        ),
        out_specs=(P("col", "row"), P("col", "row"), P("row", None, "col"), P("col", "row")),
        check_vma=False,
    )
```

```python
import jax
import jax.numpy as jnp
from jax import lax
from jax.sharding import PartitionSpec as P

BF16 = jnp.bfloat16
F32 = jnp.float32
SIDES = (4, 4, 2)


def after(array, *others):
    return lax.optimization_barrier((array,) + others)[0]


def col_shift(array, axis, step):
    moves = []
    for source in range(32):
        at = [source // 8, source // 2 % 4, source % 2]
        at[axis] = (at[axis] + step) % SIDES[axis]
        moves.append((source, at[0] * 8 + at[1] * 2 + at[2]))
    return lax.ppermute(array, "col", moves)


def row_shift(array, step):
    rows = lax.psum(1, "row")
    return lax.ppermute(array, "row", [(i, (i + step) % rows) for i in range(rows)])


def spread(array, axis):
    return jnp.stack([array] + [col_shift(array, axis, step) for step in (-1, 2, 1)])


def col_gather(array, beside):
    array = spread(spread(array, 0), 1)
    return jnp.stack([array, col_shift(after(array, beside), 2, 1)])


def row_gather(own):
    half = own.shape[1] // 256 * 128
    up, down = [own], [own]
    for _ in range(3):
        up.append(row_shift(up[-1], 1))
        down.append(row_shift(down[-1], -1))
    middle = jnp.concatenate(
        [row_shift(up[3][:, :half], 1), row_shift(down[3][:, half:], -1)], axis=1
    )
    return jnp.concatenate(down + [middle] + up[:0:-1], axis=0)


def row_sum_scatter(terms, long_up):
    size = terms.shape[0] // 8
    block = lambda b: terms[b * size : (b + 1) * size]

    def run(order, step):
        total, passed = block(order[0]), []
        for b in order[1:]:
            passed.append(row_shift(total.astype(BF16), step))
            total = passed[-1].astype(F32) + block(b)
        return row_shift(total, step), passed[0]

    up, early = run([4, 3, 2, 1] if long_up else [3, 2, 1], 1)
    down, _ = run([5, 6, 7] if long_up else [4, 5, 6, 7], -1)
    return block(0) + up + down, early


def positions(flags):
    rows, width = flags.shape
    upto = lax.broadcasted_iota(jnp.int32, (width, width), 0) <= lax.broadcasted_iota(
        jnp.int32, (width, width), 1
    )
    within = jnp.dot(flags, upto.astype(BF16), preferred_element_type=F32)
    totals = jnp.sum(flags.astype(F32), axis=1)
    before = jnp.cumsum(totals) - totals
    place = jnp.where(flags > 0, within + before[:, None] - 1.0, -1.0)
    return place.astype(jnp.int32).reshape(rows * width), jnp.sum(totals).astype(jnp.int32)


def col_order(place):
    grid = place.reshape(SIDES + (-1,))
    for axis in range(3):
        grid = jnp.concatenate([grid, grid], axis)
    me = lax.axis_index("col")
    grid = lax.dynamic_slice(grid, (me // 8, me // 2 % 4, me % 2, 0), SIDES + (grid.shape[3],))
    return grid.transpose(2, 1, 0, 3).reshape(-1)


def pick(wanted, place):
    return (wanted[:, None] == place[None, :]).astype(BF16)


def chip_sum(part, chosen, *beside):
    core = lax.axis_index("col") % 2
    half = part.shape[1] // 2
    other = lax.dynamic_slice(part, (0, (1 - core) * half), (part.shape[0], half))
    own = lax.dynamic_slice(part, (0, core * half), (part.shape[0], half))
    own = (own + col_shift(other, 2, 1)).astype(BF16)
    if beside:
        own = after(own, *beside)
    return jnp.einsum("kt,kd->td", chosen, own)


def owner_sum(spots, *beside):
    core = lax.axis_index("col") % 2
    chips = SIDES[0] * SIDES[1]
    groups = [[2 * chip + c for chip in range(chips)] for c in range(2)]
    got = lax.all_to_all(spots, "col", 0, 0, tiled=True, axis_index_groups=groups)
    got = got.reshape(chips, 2, spots.shape[0] // chips // 2, spots.shape[1])
    got = jnp.sum(got.astype(F32), axis=0).astype(BF16)
    if beside:
        got = after(got, *beside)
    away = col_shift(lax.dynamic_index_in_dim(got, 1 - core, 0, False), 2, 1)
    own = lax.dynamic_index_in_dim(got, core, 0, False)
    both = jnp.where(
        core == 0, jnp.concatenate([own, away], 1), jnp.concatenate([away, own], 1)
    )
    return both, got


def activations(gate, up):
    sig = jax.nn.sigmoid(gate)
    activated = gate * sig
    return sig, activated, (activated * up).astype(BF16)


def cotangents(gate, up, sig, activated, d_hidden):
    d_gate = (d_hidden * up * (sig + gate * sig * (1.0 - sig))).astype(BF16)
    return d_gate, (d_hidden * activated).astype(BF16)


def sum_scatter(terms):
    return lax.psum_scatter(terms, "row", scatter_dimension=0, tiled=True)


def gather(own):
    return lax.all_gather(own, "row", axis=0, tiled=True)


def per_device(tokens, modality, in_weight, down_weight, d_mixed):
    width = in_weight.shape[2]
    flat_in = in_weight.reshape(in_weight.shape[0], 2 * width)
    features = tokens.shape[1]
    flags = lax.all_gather((modality == 1).astype(BF16), "row", axis=0)
    place, count = positions(flags)
    token_place = col_order(place)
    rows_all = col_gather(tokens, flags).reshape(-1, features)
    cotangent_all = lax.all_gather(d_mixed, "col", axis=0, tiled=True)
    total = rows_all.shape[0]
    some = total // 16 * 9

    wanted = lax.axis_index("row") * (some // 8) + lax.iota(jnp.int32, some)
    wanted = jnp.where(wanted >= some, wanted - some, wanted)
    rows = jnp.dot(pick(wanted, token_place), rows_all)
    projected, early = row_sum_scatter(jnp.dot(rows, flat_in, preferred_element_type=F32), True)
    gate, up = projected[:, :width], projected[:, width:]
    cotangent_all = after(cotangent_all, early)
    chosen = pick(wanted, place)
    canon = pick(lax.iota(jnp.int32, some), place)
    d_hidden = sum_scatter(
        jnp.einsum(
            "td,fd->tf", jnp.dot(canon, cotangent_all), down_weight, preferred_element_type=F32
        )
    )
    sig, activated, hidden = activations(gate, up)
    hidden_all = row_gather(hidden)
    mixed_spots = chip_sum(jnp.dot(hidden_all, down_weight, preferred_element_type=F32), chosen)
    mixed, mixed_sum = owner_sum(mixed_spots)
    cotangent = jnp.dot(chosen, cotangent_all)
    d_down = jnp.einsum("tf,td->fd", hidden_all, cotangent, preferred_element_type=F32).astype(BF16)
    d_gate, d_up = cotangents(gate, up, sig, activated, d_hidden)
    d_projected = gather(jnp.concatenate([d_gate, d_up], 1))
    d_projected = after(d_projected, mixed_spots)
    d_spots = chip_sum(
        jnp.einsum("tk,dk->td", d_projected, flat_in, preferred_element_type=F32),
        canon,
        mixed_sum,
        d_down,
    )
    canon_rows = jnp.dot(pick(lax.iota(jnp.int32, some), token_place), rows_all)
    d_in = jnp.einsum("td,tk->dk", canon_rows, d_projected, preferred_element_type=F32)
    d_in = d_in.reshape(in_weight.shape).astype(BF16)
    d_tokens, _ = owner_sum(d_spots, d_in)

    rest = total - some

    def more(carry):
        return carry[0] < count

    def step(carry):
        start, mixed, d_down, d_in, d_tokens = carry
        wanted = start + lax.iota(jnp.int32, rest)
        chosen = pick(wanted, place)
        rows = jnp.dot(pick(wanted, token_place), rows_all)
        cotangent = jnp.dot(chosen, cotangent_all)
        projected = sum_scatter(jnp.dot(rows, flat_in, preferred_element_type=F32))
        d_hidden = sum_scatter(
            jnp.einsum("td,fd->tf", cotangent, down_weight, preferred_element_type=F32)
        )
        gate, up = projected[:, :width], projected[:, width:]
        sig, activated, hidden = activations(gate, up)
        d_projected = jnp.concatenate(cotangents(gate, up, sig, activated, d_hidden), 1)
        hidden, d_projected = gather(hidden), gather(d_projected)
        mixed += owner_sum(
            chip_sum(jnp.dot(hidden, down_weight, preferred_element_type=F32), chosen)
        )[0]
        d_tokens += owner_sum(
            chip_sum(
                jnp.einsum("tk,dk->td", d_projected, flat_in, preferred_element_type=F32), chosen
            )
        )[0]
        add = jnp.einsum("tf,td->fd", hidden, cotangent, preferred_element_type=F32)
        d_down = (d_down.astype(F32) + add).astype(BF16)
        add = jnp.einsum("td,tk->dk", rows, d_projected, preferred_element_type=F32)
        d_in = (d_in.astype(F32) + add.reshape(d_in.shape)).astype(BF16)
        return start + rest, mixed, d_down, d_in, d_tokens

    carry = (jnp.int32(some), mixed, d_down, d_in, d_tokens)
    return lax.while_loop(more, step, carry)[1:]


def solution(mesh):
    return jax.shard_map(
        per_device,
        mesh=mesh,
        in_specs=(
            P("col", "row"),
            P("row"),
            P("row", None, "col"),
            P("col", "row"),
            P("col", "row"),
        ),
        out_specs=(P("col", "row"), P("col", "row"), P("row", None, "col"), P("col", "row")),
        check_vma=False,
    )
```
